32 devices in a mesh: pipe: 4 (over y, x), expert: 2 (over core), dp: 4 (over z).
Axes of the slice: x: 2, y: 2, z: 4, core: 2. Of those that a mesh axis runs over, the one named last changes fastest.
Arguments:
- hidden_in: bfloat16 [4096, 6144], P(('pipe', 'expert', 'dp'))
- norm_gain: float32 [4, 6144], P('pipe'), may hold values from 0.1 to 1.9
- w_gate: bfloat16 [4, 6144, 8192], P('pipe', None, ('expert', 'dp')), may hold values from -0.078125 to 0.078125
- w_up: bfloat16 [4, 6144, 8192], P('pipe', None, ('expert', 'dp')), may hold values from -0.078125 to 0.078125
- w_down: bfloat16 [4, 8192, 6144], P('pipe', ('expert', 'dp')), may hold values from -0.0625 to 0.0625
- expert_ids: int32 [4096, 2], P(('pipe', 'expert', 'dp')), may hold values from 0 to 7, as said below
- gate_weights: float32 [4096, 2], P(('pipe', 'expert', 'dp')), may hold values from 0.25 to 1
Outputs:
- passed_on: bfloat16 [4096, 6144], P(('pipe', 'expert', 'dp'))
The draws below stay inside these ranges and needn't reach their ends.
Inputs may be any that keep to these rules, and one draw needn't show every extreme that they name: `expert_ids`: the two ids of a row differ. In every aligned block of 128 rows (the rows of one device) at most 64 rows name expert 0, and in each section's 8 blocks at least one block has 64 such rows; the 8 blocks of one section hold exactly 256 rows that name expert 0.
All inputs are finite; a program needn't handle non-finite values.
Results may differ from the reference program's by a relative error of at most 0.0045.
Values may be sent and summed in bfloat16 or wider, within the bound.
No kernel may reach another device: no remote copies, remote signals or barrier semaphores. Data moves between devices by JAX's collectives and lax.ppermute only.
A program may use at most 192 MiB of HBM per device.

```python
import math
import jax
import jax.numpy as jnp
from jax import lax

D = 6144
FF_WIN = 8192
EXPERTS = 8
TOP = 2
TOK_DEV = 128
CAP = 64
GROUP = 8
SECTIONS = 4
TOKENS = 4096


def draw_hidden_in(key, part):
    key = jax.random.fold_in(key, 5)
    key_base, key_row, key_col = jax.random.split(key, 3)
    base = jax.random.normal(key_base, (TOKENS, D), jnp.float32)
    row_scale = jnp.exp(jax.random.uniform(key_row, (TOKENS, 1), jnp.float32, math.log(0.3), math.log(3.0)))
    col_scale = jnp.exp(jax.random.uniform(key_col, (1, D), jnp.float32, math.log(0.3), math.log(3.0)))
    return (base * row_scale * col_scale).astype(jnp.bfloat16)


def draw_expert_ids(key, part):
    key = jax.random.fold_in(key, 11)
    keys = jax.random.split(key, 6)
    blocks = TOKENS // TOK_DEV
    section_count = blocks // GROUP
    half = CAP // 2
    spread = jax.random.randint(keys[0], (section_count, GROUP // 2), 0, half + 1)
    spread = spread.at[:, 0].set(half)
    paired = jnp.stack([half + spread, half - spread], axis=-1).reshape(section_count, GROUP)
    orders = jax.vmap(lambda k: jax.random.permutation(k, GROUP))(jax.random.split(keys[1], section_count))
    counts = jnp.take_along_axis(paired, orders, axis=1).reshape(blocks)
    ranks = jax.vmap(lambda k: jax.random.permutation(k, TOK_DEV))(jax.random.split(keys[2], blocks))
    chosen = ranks < counts[:, None]
    other = jax.random.randint(keys[3], (blocks, TOK_DEV), 1, EXPERTS)
    offset = jax.random.randint(keys[4], (blocks, TOK_DEV), 1, EXPERTS - 1)
    second = 1 + (other - 1 + offset) % (EXPERTS - 1)
    flip = jax.random.randint(keys[5], (blocks, TOK_DEV), 0, 2)
    first_id = jnp.where(chosen & (flip == 0), 0, other)
    last_id = jnp.where(chosen, jnp.where(flip == 1, 0, other), second)
    return jnp.stack([first_id, last_id], axis=-1).reshape(TOKENS, TOP).astype(jnp.int32)


def steps_of(stream_key, dims, cuts, least, high):
    level = 1.0
    for position, shards_of in cuts:
        steps = jax.random.uniform(jax.random.fold_in(jax.random.fold_in(stream_key, 6), position), (shards_of,), jnp.float32, least / len(cuts), high / len(cuts))
        level = level * jnp.repeat(jnp.exp(steps), dims[position] // shards_of).reshape((-1,) + (1,) * (len(dims) - 1 - position))
    return level


def centred(rng, shape, width, reach, shards=(), held_as=jnp.bfloat16):
    factor_of = steps_of(rng, shape, shards, -0.22, 0.18) if shards else 1.0
    entries = jax.random.normal(rng, shape, jnp.float32) * width * factor_of
    return jnp.minimum(jnp.maximum(entries, -reach), reach).astype(held_as)


def setup_inputs(seed: int = 0) -> dict:
    key_list = jax.random.split(jax.random.key(seed), 8)
    hidden_in = draw_hidden_in(jax.random.fold_in(key_list[7], 71), 0)
    norm_gain = jnp.clip(1.0 + 0.18 * jax.random.normal(key_list[1], (SECTIONS, D), jnp.float32), 0.1, 1.9)
    w_gate = centred(key_list[2], (SECTIONS, D, FF_WIN), D ** -0.5, 0.078125, ((0, 4), (2, 8)))
    w_up = centred(key_list[3], (SECTIONS, D, FF_WIN), D ** -0.5, 0.078125, ((0, 4), (2, 8)))
    w_down = centred(key_list[4], (SECTIONS, FF_WIN, D), FF_WIN ** -0.5, 0.0625, ((0, 4), (1, 8)))
    expert_ids = draw_expert_ids(jax.random.fold_in(key_list[7], 71), 0)
    gate_weights = jnp.clip(0.25 + 0.75 * jax.random.uniform(key_list[6], (TOKENS, TOP), jnp.float32) ** steps_of(key_list[6], (TOKENS, TOP), ((0, 32),), -0.2, 0.2), 0.25, 1.0)
    return dict(hidden_in=hidden_in, norm_gain=norm_gain, w_gate=w_gate, w_up=w_up, w_down=w_down, expert_ids=expert_ids, gate_weights=gate_weights)


def rms_scale(values_in, gain):
    values = values_in.astype(jnp.float32)
    mean_sq = lax.optimization_barrier(jnp.mean(values * values, axis=-1, keepdims=True))
    return (values * lax.rsqrt(mean_sq + 1e-05) * gain).astype(jnp.bfloat16)

def expert_rows(normed, gate_matrix, up_matrix, down_matrix):
    gate = jnp.dot(normed, gate_matrix, preferred_element_type=jnp.float32)
    up_values = jnp.dot(normed, up_matrix, preferred_element_type=jnp.float32)
    hidden = (jax.nn.silu(gate) * up_values).astype(jnp.bfloat16)
    return jnp.dot(hidden, down_matrix, preferred_element_type=jnp.float32)

def reference(hidden_in, norm_gain, w_gate, w_up, w_down, expert_ids, gate_weights):
    section_rows = GROUP * TOK_DEV
    routed_count = GROUP * CAP // 2
    inputs = hidden_in.reshape(SECTIONS, section_rows, D)
    id_blocks = expert_ids.reshape(SECTIONS, section_rows, TOP)
    gate_blocks = gate_weights.reshape(SECTIONS, section_rows, TOP)

    def one_section(section_args):
        block, gain, gate_matrix, up_matrix, down_matrix, id_rows, gate_rows = section_args
        normed = rms_scale(block, gain)
        chosen = id_rows == 0
        routed = jnp.any(chosen, axis=1)
        own_weight = lax.optimization_barrier(jnp.sum(jnp.where(chosen, gate_rows, 0.0), axis=1))
        order = jnp.argsort(jnp.where(routed, 0, 1).astype(jnp.int32), stable=True)[:routed_count].astype(jnp.int32)
        result = expert_rows(normed[order], gate_matrix, up_matrix, down_matrix)
        branch = jnp.zeros((section_rows, D), result.dtype).at[order].set(result)
        combined = block.astype(jnp.float32) + own_weight[:, None] * branch
        return combined.astype(jnp.bfloat16)
    outputs = lax.map(one_section, (inputs, norm_gain, w_gate, w_up, w_down, id_blocks, gate_blocks))
    return jnp.roll(outputs, 1, axis=0).reshape(SECTIONS * section_rows, D)
```

```python
import functools

import jax
import jax.numpy as jnp
from jax import lax
from jax.experimental import pallas as pl
from jax.experimental.pallas import tpu as pltpu
from jax.sharding import PartitionSpec as P

MIB = 2**20
VMEM_HIDDEN = 34
VMEM_DOWN = 24
PIECES = 4


def next_section(block):
    count = lax.axis_size("pipe")
    return lax.ppermute(block, "pipe", [(i, (i + 1) % count) for i in range(count)])


def other_core(block):
    count = lax.axis_size("expert")
    return lax.ppermute(block, "expert", [(i, (i + 1) % count) for i in range(count)])


def routing_rows(ids, weights):
    rows = ids.shape[1]
    chosen = ids == 0
    routed = jnp.max(jnp.where(chosen, 1.0, 0.0), axis=0, keepdims=True)
    own = jnp.sum(jnp.where(chosen, weights, 0.0), axis=0, keepdims=True)
    before = lax.broadcasted_iota(jnp.int32, (rows, rows), 0)
    after = lax.broadcasted_iota(jnp.int32, (rows, rows), 1)
    upper = jnp.where(before <= after, 1.0, 0.0).astype(jnp.bfloat16)
    counted = jnp.dot(
        jnp.broadcast_to(routed, (16, rows)).astype(jnp.bfloat16), upper, preferred_element_type=jnp.float32
    )[0:1]
    place = jnp.where(routed > 0.5, counted - 1.0, -1.0)
    return place, own


def as_column(row):
    size = row.shape[1]
    on_row = lax.broadcasted_iota(jnp.int32, (size, size), 0)
    on_col = lax.broadcasted_iota(jnp.int32, (size, size), 1)
    return jnp.sum(jnp.where(on_row == on_col, row, 0.0), axis=1, keepdims=True)


def pack_kernel(step, sizes, x_hbm, gain_hbm, ids_hbm, weights_hbm, meta_ref, *refs):
    packed, (values, x_ref, gain_ref, ids_ref, weights_ref, sem) = refs[: len(sizes)], refs[len(sizes) :]
    copies = [
        pltpu.make_async_copy(source, target, sem.at[i])
        for i, (source, target) in enumerate(
            [(ids_hbm, ids_ref), (weights_hbm, weights_ref), (gain_hbm, gain_ref), (x_hbm, x_ref)]
        )
    ]
    for copy in copies:
        copy.start()
    for copy in copies[:2]:
        copy.wait()
    rows, width = x_ref.shape
    slots = values.shape[0]
    place, own = routing_rows(ids_ref[...], weights_ref[...])
    meta_ref[0:1] = place
    meta_ref[1:2] = own
    slot = lax.broadcasted_iota(jnp.int32, (slots, rows), 0).astype(jnp.float32)
    picked = jnp.where(slot == place, 1.0, 0.0).astype(jnp.bfloat16)
    for copy in copies[2:]:
        copy.wait()
    total = jnp.zeros((slots, 1), jnp.float32)
    for start in range(0, width, step):
        part = jnp.dot(picked, x_ref[:, start : start + step], preferred_element_type=jnp.float32)
        values[:, start : start + step] = part
        total += jnp.sum(part * part, axis=1, keepdims=True)
    scale = lax.rsqrt(total / width + 1e-05)
    for start in range(0, width, step):
        normed = values[:, start : start + step] * scale * gain_ref[:, start : start + step]
        normed = normed.astype(jnp.bfloat16)
        first = 0
        for size, out in zip(sizes, packed):
            out[:, start : start + step] = normed[first : first + size]
            first += size


def pack(x, gain, ids, weights, sizes):
    rows, width = x.shape
    slots = sum(sizes)
    vmem = pl.BlockSpec(memory_space=pltpu.VMEM)
    stays = pl.BlockSpec(memory_space=pltpu.HBM)
    return pl.pallas_call(
        functools.partial(pack_kernel, 512, sizes),
        out_shape=[jax.ShapeDtypeStruct((2, rows), jnp.float32)]
        + [jax.ShapeDtypeStruct((size, width), jnp.bfloat16) for size in sizes],
        in_specs=[stays] * 4,
        out_specs=[vmem] * (len(sizes) + 1),
        scratch_shapes=[
            pltpu.VMEM((slots, width), jnp.float32),
            pltpu.VMEM(x.shape, x.dtype),
            pltpu.VMEM(gain.shape, gain.dtype),
            pltpu.VMEM(ids.shape, ids.dtype),
            pltpu.VMEM(weights.shape, weights.dtype),
            pltpu.SemaphoreType.DMA((4,)),
        ],
        compiler_params=pltpu.CompilerParams(vmem_limit_bytes=8 * MIB),
        cost_estimate=pl.CostEstimate(flops=2 * slots * rows * width, bytes_accessed=3 * rows * width, transcendentals=slots),
        name="pack_rows",
    )(*(pltpu.with_memory_space_constraint(each, pltpu.HBM) for each in (x, gain, ids, weights)))


def combine_kernel(step, sizes, pieces, meta_ref, *refs):
    inputs, refs = refs[:pieces], refs[pieces:]
    arrived, (out, sums) = refs[:-2], refs[-2:]
    rows, width = out.shape
    each = rows // pieces
    first = 0
    for k, size in enumerate(sizes):
        total = sum(part[...].astype(jnp.float32) for part in arrived[3 * k : 3 * k + 3])
        sums[first : first + size] = total.astype(jnp.bfloat16)
        first += size
    place, own = as_column(meta_ref[0:1]), as_column(meta_ref[1:2])
    slot = lax.broadcasted_iota(jnp.int32, (rows, first), 1).astype(jnp.float32)
    spread = jnp.where(slot == place, 1.0, 0.0).astype(jnp.bfloat16)
    for start in range(0, width, step):
        branch = own * jnp.dot(spread, sums[:, start : start + step], preferred_element_type=jnp.float32)
        for p, piece in enumerate(inputs):
            mine = slice(p * each, (p + 1) * each)
            x = piece[:, start : start + step].astype(jnp.float32)
            out[mine, start : start + step] = (x + branch[mine]).astype(jnp.bfloat16)


def combine(inputs, meta, arrived):
    rows, width = meta.shape[1], inputs[0].shape[1]
    sizes = [part.shape[0] for part in arrived[::3]]
    vmem = pl.BlockSpec(memory_space=pltpu.VMEM)
    return pl.pallas_call(
        functools.partial(combine_kernel, 512, sizes, len(inputs)),
        out_shape=jax.ShapeDtypeStruct((rows, width), jnp.bfloat16),
        in_specs=[vmem] * (1 + len(inputs) + len(arrived)),
        out_specs=vmem,
        scratch_shapes=[pltpu.VMEM((sum(sizes), width), jnp.bfloat16)],
        compiler_params=pltpu.CompilerParams(vmem_limit_bytes=8 * MIB),
        cost_estimate=pl.CostEstimate(flops=rows * rows * width, bytes_accessed=5 * rows * width, transcendentals=0),
        name="combine_rows",
    )(meta, *inputs, *arrived)


def hidden_kernel(cols, parts, *refs):
    blocks, (gate_m, up_m, out, x_v, wide_v, wide_sem) = refs[:8], refs[8:]
    rows = blocks[0].shape[0]
    tiles = gate_m.shape[1] // cols

    depth = x_v.shape[1] // parts

    def pair_copies(t, slot, part):
        at, rows_at = pl.ds(t * cols, cols), pl.ds(part * depth, depth)
        return [
            pltpu.make_async_copy(gate_m.at[rows_at, at], wide_v.at[slot, rows_at, pl.ds(0, cols)], wide_sem.at[slot, part, 0]),
            pltpu.make_async_copy(up_m.at[rows_at, at], wide_v.at[slot, rows_at, pl.ds(cols, cols)], wide_sem.at[slot, part, 1]),
        ]

    for t in range(tiles):
        for part in range(parts):
            for copy in pair_copies(t, t, part):
                copy.start()
    for i, block in enumerate(blocks):
        x_v[i * rows : (i + 1) * rows] = block[...]

    for t in range(tiles):
        for part in range(parts):
            for copy in pair_copies(t, t, part):
                copy.wait()
            if t == 0:
                k = slice(part * depth, (part + 1) * depth)
                piece = jnp.dot(x_v[:, k], wide_v[t, k], preferred_element_type=jnp.float32)
                both = piece if part == 0 else both + piece
        if t > 0:
            both = jnp.dot(x_v[...], wide_v[t], preferred_element_type=jnp.float32)
        gate, up = both[:, :cols], both[:, cols:]
        out[:, t * cols : (t + 1) * cols] = (gate / (1.0 + jnp.exp(-gate)) * up).astype(jnp.bfloat16)


def down_kernel(cols, hidden, down_m, *refs):
    outs, (down_v, down_sem) = refs[:4], refs[4:]
    width = down_m.shape[1]
    tiles, slots = width // cols, down_v.shape[0]

    def down_copy(t, slot):
        return pltpu.make_async_copy(down_m.at[:, pl.ds(t * cols, cols)], down_v.at[slot], down_sem.at[slot])

    for t in range(slots):
        down_copy(t, t).start()
    for t in range(tiles):
        slot = t % slots
        down_copy(t, slot).wait()
        total = jnp.dot(hidden[...], down_v[slot], preferred_element_type=jnp.float32).astype(jnp.bfloat16)
        first = 0
        for out in outs:
            out[:, t * cols : (t + 1) * cols] = total[first : first + out.shape[0]]
            first += out.shape[0]
        if t + slots < tiles:
            down_copy(t + slots, slot).start()


def in_hbm(matrix):
    return pltpu.with_memory_space_constraint(matrix, pltpu.HBM)


def expert_hidden(blocks, gate_m, up_m):
    rows, width = blocks[0].shape
    hidden = gate_m.shape[1]
    cols, parts = 256, 4
    vmem, stays = pl.BlockSpec(memory_space=pltpu.VMEM), pl.BlockSpec(memory_space=pltpu.HBM)
    return pl.pallas_call(
        functools.partial(hidden_kernel, cols, parts),
        out_shape=jax.ShapeDtypeStruct((8 * rows, hidden), jnp.bfloat16),
        in_specs=[vmem] * 8 + [stays] * 2,
        out_specs=vmem,
        scratch_shapes=[
            pltpu.VMEM((8 * rows, width), jnp.bfloat16),
            pltpu.VMEM((hidden // cols, width, 2 * cols), jnp.bfloat16),
            pltpu.SemaphoreType.DMA((hidden // cols, parts, 2)),
        ],
        compiler_params=pltpu.CompilerParams(vmem_limit_bytes=VMEM_HIDDEN * MIB),
        cost_estimate=pl.CostEstimate(
            flops=32 * rows * width * hidden,
            bytes_accessed=4 * width * hidden + 16 * rows * width,
            transcendentals=8 * rows * hidden,
        ),
        name="expert_hidden",
    )(*blocks, in_hbm(gate_m), in_hbm(up_m))


def expert_down(hidden, down_m):
    rows, width = hidden.shape[0] // 8, down_m.shape[1]
    cols = 1024
    vmem, stays = pl.BlockSpec(memory_space=pltpu.VMEM), pl.BlockSpec(memory_space=pltpu.HBM)
    first, rest = [jax.ShapeDtypeStruct((count * rows, width), jnp.bfloat16) for count in (1, 3)]
    return pl.pallas_call(
        functools.partial(down_kernel, cols),
        out_shape=[first, rest, first, rest],
        in_specs=[vmem, stays],
        out_specs=[vmem] * 4,
        scratch_shapes=[
            pltpu.VMEM((width // cols, down_m.shape[0], cols), jnp.bfloat16),
            pltpu.SemaphoreType.DMA((width // cols,)),
        ],
        compiler_params=pltpu.CompilerParams(vmem_limit_bytes=VMEM_DOWN * MIB),
        cost_estimate=pl.CostEstimate(
            flops=16 * rows * width * down_m.shape[0],
            bytes_accessed=2 * width * down_m.shape[0] + 32 * rows * width,
            transcendentals=0,
        ),
        name="expert_down",
    )(hidden, in_hbm(down_m))


def add(*terms):
    total = terms[0].astype(jnp.float32)
    for term in terms[1:]:
        total += term.astype(jnp.float32)
    return total.astype(jnp.bfloat16)


def after(block, *earlier):
    return lax.optimization_barrier((block, *earlier))[0]


def route(block, target, cores=(0, 1)):
    sections, chips = lax.axis_size("pipe"), lax.axis_size("dp")
    index = lambda section, core, chip: ((section % sections) * 2 + core) * chips + chip
    pairs = [
        (index(section, core, chip), index(*target(section, core, chip)))
        for section in range(sections)
        for core in cores
        for chip in range(chips)
    ]
    return lax.ppermute(block, ("pipe", "expert", "dp"), pairs)


def chip(mask):
    return lambda s, c, z: (s, c, z ^ mask)


def next_chip(mask):
    return lambda s, c, z: (s + 1, c, z ^ mask)


def per_device(hidden_in, norm_gain, w_gate, w_up, w_down, expert_ids, gate_weights):
    rows = hidden_in.shape[0]
    size, each = rows // 4, rows // PIECES
    meta, *packed = pack(hidden_in, norm_gain, expert_ids.T, gate_weights.T, [size, size // 2, size // 2])
    meta_before = next_section(meta)
    halves = [packed[0], jnp.concatenate(packed[1:], axis=0)]
    swapped = other_core(packed[0])
    early = after(hidden_in, swapped)
    inputs = [next_section(early[p * each : (p + 1) * each]) for p in range(PIECES)]

    def expert_hidden_of(blocks, theirs):
        return expert_hidden(blocks + theirs, w_gate[0], w_up[0])

    def scatter(terms, wait_for_own):
        keep_first, keep_rest, send_first, send_rest = terms
        partner = route(add(keep_first, other_core(send_first)), chip(1))
        rest = add(keep_rest, other_core(send_rest))
        stays = route(rest[2 * size :], next_chip(0))
        across = route(rest[size : 2 * size], next_chip(1))
        if wait_for_own:
            partner = after(partner, stays)
        return [stays, across, route(add(rest[:size], partner), next_chip(3))]

    cross, near = route(packed[0], chip(3)), route(after(packed[0], swapped), chip(1))
    far = route(after(cross, *inputs[:2]), chip(1))
    cross_swapped = other_core(cross)
    cross_next = [route(after(block, cross_swapped), chip(3)) for block in packed[1:]]
    near_next = route(after(halves[1], cross_swapped), chip(1))
    mine = [far, cross, near, after(packed[0], inputs[2], cross_next[0], meta_before)]
    hidden = expert_hidden_of(mine, [other_core(far), cross_swapped, other_core(near), swapped])
    cross_next = jnp.concatenate([after(block, hidden) for block in cross_next], axis=0)
    far_next = route(after(cross_next, hidden), chip(1))
    terms = expert_down(after(hidden, near_next, inputs[3]), w_down[0])
    arrived = scatter([after(term, far_next) for term in terms], True)

    mine = [far_next, cross_next, near_next, halves[1]]
    hidden = expert_hidden_of(mine, [other_core(block) for block in mine])
    keep_first, keep_rest, send_first, send_rest = expert_down(hidden, w_down[0])
    send_first, send_rest = after(send_first, *arrived), after(send_rest, *arrived)
    arrived += scatter([keep_first, keep_rest, send_first, send_rest], False)
    return combine(inputs, meta_before, arrived)


def rms_scale(values_in, gain):
    values = values_in.astype(jnp.float32)
    mean_sq = jnp.mean(values * values, axis=-1, keepdims=True)
    return (values * lax.rsqrt(mean_sq + 1e-05) * gain).astype(jnp.bfloat16)


def expert_rows(normed, gate_matrix, up_matrix, down_matrix):
    gate = jnp.dot(normed, gate_matrix, preferred_element_type=jnp.float32)
    up_values = jnp.dot(normed, up_matrix, preferred_element_type=jnp.float32)
    hidden = (jax.nn.silu(gate) * up_values).astype(jnp.bfloat16)
    return jnp.dot(hidden, down_matrix, preferred_element_type=jnp.float32)


def per_device_any(hidden_in, norm_gain, w_gate, w_up, w_down, expert_ids, gate_weights):
    row_count = hidden_in.shape[0]
    capacity = row_count // 2
    normed = rms_scale(hidden_in, norm_gain[0])
    chosen = expert_ids == 0
    routed = jnp.any(chosen, axis=1)
    own_weight = jnp.sum(jnp.where(chosen, gate_weights, 0.0), axis=1)
    position = jnp.cumsum(routed.astype(jnp.int32)) - 1
    slot_grid = lax.broadcasted_iota(jnp.int32, (capacity, row_count), 0)
    token_grid = lax.broadcasted_iota(jnp.int32, (capacity, row_count), 1)
    picked = (position[None, :] == slot_grid) & routed[None, :]
    source = jnp.sum(jnp.where(picked, token_grid, 0), axis=1)
    filled = jnp.any(picked, axis=1)
    packed = jnp.where(
        filled[:, None], jnp.take(normed, source, axis=0), jnp.zeros_like(normed[:1])
    )
    gate_matrix = w_gate[0]
    up_matrix = w_up[0]
    down_matrix = w_down[0]
    terms = expert_rows(
        lax.all_gather(packed, ("expert", "dp"), axis=0, tiled=True),
        gate_matrix,
        up_matrix,
        down_matrix,
    )
    own_rows = lax.psum_scatter(
        terms.astype(jnp.bfloat16), ("expert", "dp"), scatter_dimension=0, tiled=True
    ).astype(jnp.float32)
    back = jnp.take(own_rows, jnp.clip(position, 0, capacity - 1), axis=0)
    branch = jnp.where(routed[:, None], back, 0.0)
    combined = (hidden_in.astype(jnp.float32) + own_weight[:, None] * branch).astype(jnp.bfloat16)
    return next_section(combined)


def solution(mesh):
    paired = mesh.shape["dp"] == 4 and mesh.shape["expert"] == 2
    return jax.shard_map(
        per_device if paired else per_device_any,
        mesh=mesh,
        in_specs=(
            P(("pipe", "expert", "dp"), None),
            P("pipe", None),
            P("pipe", None, ("expert", "dp")),
            P("pipe", None, ("expert", "dp")),
            P("pipe", ("expert", "dp"), None),
            P(("pipe", "expert", "dp"), None),
            P(("pipe", "expert", "dp"), None),
        ),
        out_specs=P(("pipe", "expert", "dp"), None),
        check_vma=False,
    )
```

```python
import functools

import jax
import jax.numpy as jnp
from jax import lax
from jax.experimental import pallas as pl
from jax.experimental.pallas import tpu as pltpu
from jax.sharding import PartitionSpec as P

MIB = 2**20
VMEM_HIDDEN = 34
VMEM_DOWN = 24
PIECES, PIECES_OF = (2, 1, 2, 3), 8


def next_section(block):
    count = lax.axis_size("pipe")
    return lax.ppermute(block, "pipe", [(i, (i + 1) % count) for i in range(count)])


def other_core(block):
    count = lax.axis_size("expert")
    return lax.ppermute(block, "expert", [(i, (i + 1) % count) for i in range(count)])


def routing_rows(ids, weights):
    rows = ids.shape[1]
    chosen = ids == 0
    routed = jnp.max(jnp.where(chosen, 1.0, 0.0), axis=0, keepdims=True)
    own = jnp.sum(jnp.where(chosen, weights, 0.0), axis=0, keepdims=True)
    before = lax.broadcasted_iota(jnp.int32, (rows, rows), 0)
    after = lax.broadcasted_iota(jnp.int32, (rows, rows), 1)
    upper = jnp.where(before <= after, 1.0, 0.0).astype(jnp.bfloat16)
    counted = jnp.dot(
        jnp.broadcast_to(routed, (16, rows)).astype(jnp.bfloat16), upper, preferred_element_type=jnp.float32
    )[0:1]
    place = jnp.where(routed > 0.5, counted - 1.0, -1.0)
    return place, own


def as_column(row):
    size = row.shape[1]
    on_row = lax.broadcasted_iota(jnp.int32, (size, size), 0)
    on_col = lax.broadcasted_iota(jnp.int32, (size, size), 1)
    return jnp.sum(jnp.where(on_row == on_col, row, 0.0), axis=1, keepdims=True)


def pack_kernel(step, sizes, x_hbm, gain_hbm, ids_hbm, weights_hbm, meta_ref, *refs):
    packed, (values, x_ref, gain_ref, ids_ref, weights_ref, sem) = refs[: len(sizes)], refs[len(sizes) :]
    copies = [
        pltpu.make_async_copy(source, target, sem.at[i])
        for i, (source, target) in enumerate(
            [(ids_hbm, ids_ref), (weights_hbm, weights_ref), (gain_hbm, gain_ref), (x_hbm, x_ref)]
        )
    ]
    for copy in copies:
        copy.start()
    for copy in copies[:2]:
        copy.wait()
    rows, width = x_ref.shape
    slots = values.shape[0]
    place, own = routing_rows(ids_ref[...], weights_ref[...])
    meta_ref[0:1] = place
    meta_ref[1:2] = own
    slot = lax.broadcasted_iota(jnp.int32, (slots, rows), 0).astype(jnp.float32)
    picked = jnp.where(slot == place, 1.0, 0.0).astype(jnp.bfloat16)
    for copy in copies[2:]:
        copy.wait()
    total = jnp.zeros((slots, 1), jnp.float32)
    for start in range(0, width, step):
        part = jnp.dot(picked, x_ref[:, start : start + step], preferred_element_type=jnp.float32)
        values[:, start : start + step] = part
        total += jnp.sum(part * part, axis=1, keepdims=True)
    scale = lax.rsqrt(total / width + 1e-05)
    for start in range(0, width, step):
        normed = values[:, start : start + step] * scale * gain_ref[:, start : start + step]
        normed = normed.astype(jnp.bfloat16)
        first = 0
        for size, out in zip(sizes, packed):
            out[:, start : start + step] = normed[first : first + size]
            first += size


def pack(x, gain, ids, weights, sizes):
    rows, width = x.shape
    slots = sum(sizes)
    vmem = pl.BlockSpec(memory_space=pltpu.VMEM)
    stays = pl.BlockSpec(memory_space=pltpu.HBM)
    return pl.pallas_call(
        functools.partial(pack_kernel, 512, sizes),
        out_shape=[jax.ShapeDtypeStruct((2, rows), jnp.float32)]
        + [jax.ShapeDtypeStruct((size, width), jnp.bfloat16) for size in sizes],
        in_specs=[stays] * 4,
        out_specs=[vmem] * (len(sizes) + 1),
        scratch_shapes=[
            pltpu.VMEM((slots, width), jnp.float32),
            pltpu.VMEM(x.shape, x.dtype),
            pltpu.VMEM(gain.shape, gain.dtype),
            pltpu.VMEM(ids.shape, ids.dtype),
            pltpu.VMEM(weights.shape, weights.dtype),
            pltpu.SemaphoreType.DMA((4,)),
        ],
        compiler_params=pltpu.CompilerParams(vmem_limit_bytes=8 * MIB),
        cost_estimate=pl.CostEstimate(flops=2 * slots * rows * width, bytes_accessed=3 * rows * width, transcendentals=slots),
        name="pack_rows",
    )(*(pltpu.with_memory_space_constraint(each, pltpu.HBM) for each in (x, gain, ids, weights)))


def combine_kernel(step, sizes, pieces, meta_ref, *refs):
    inputs, refs = refs[:pieces], refs[pieces:]
    arrived, (out, sums) = refs[:-2], refs[-2:]
    rows, width = out.shape
    first = 0
    for k, size in enumerate(sizes):
        total = sum(part[...].astype(jnp.float32) for part in arrived[3 * k : 3 * k + 3])
        sums[first : first + size] = total.astype(jnp.bfloat16)
        first += size
    place, own = as_column(meta_ref[0:1]), as_column(meta_ref[1:2])
    slot = lax.broadcasted_iota(jnp.int32, (rows, first), 1).astype(jnp.float32)
    spread = jnp.where(slot == place, 1.0, 0.0).astype(jnp.bfloat16)
    for start in range(0, width, step):
        branch = own * jnp.dot(spread, sums[:, start : start + step], preferred_element_type=jnp.float32)
        done = 0
        for piece in inputs:
            mine = slice(done, done + piece.shape[0])
            x = piece[:, start : start + step].astype(jnp.float32)
            out[mine, start : start + step] = (x + branch[mine]).astype(jnp.bfloat16)
            done += piece.shape[0]


def combine(inputs, meta, arrived):
    rows, width = meta.shape[1], inputs[0].shape[1]
    sizes = [part.shape[0] for part in arrived[::3]]
    vmem = pl.BlockSpec(memory_space=pltpu.VMEM)
    return pl.pallas_call(
        functools.partial(combine_kernel, 512, sizes, len(inputs)),
        out_shape=jax.ShapeDtypeStruct((rows, width), jnp.bfloat16),
        in_specs=[vmem] * (1 + len(inputs) + len(arrived)),
        out_specs=vmem,
        scratch_shapes=[pltpu.VMEM((sum(sizes), width), jnp.bfloat16)],
        compiler_params=pltpu.CompilerParams(vmem_limit_bytes=8 * MIB),
        cost_estimate=pl.CostEstimate(flops=rows * rows * width, bytes_accessed=5 * rows * width, transcendentals=0),
        name="combine_rows",
    )(meta, *inputs, *arrived)


def hidden_kernel(cols, parts, *refs):
    blocks, (gate_m, up_m, out, x_v, wide_v, wide_sem) = refs[:8], refs[8:]
    rows = blocks[0].shape[0]
    tiles = gate_m.shape[1] // cols

    depth = x_v.shape[1] // parts

    def pair_copies(t, slot, part):
        at, rows_at = pl.ds(t * cols, cols), pl.ds(part * depth, depth)
        return [
            pltpu.make_async_copy(gate_m.at[rows_at, at], wide_v.at[slot, rows_at, pl.ds(0, cols)], wide_sem.at[slot, part, 0]),
            pltpu.make_async_copy(up_m.at[rows_at, at], wide_v.at[slot, rows_at, pl.ds(cols, cols)], wide_sem.at[slot, part, 1]),
        ]

    for t in range(tiles):
        for part in range(parts):
            for copy in pair_copies(t, t, part):
                copy.start()
    for i, block in enumerate(blocks):
        x_v[i * rows : (i + 1) * rows] = block[...]

    for t in range(tiles):
        for part in range(parts):
            for copy in pair_copies(t, t, part):
                copy.wait()
            if t == 0:
                k = slice(part * depth, (part + 1) * depth)
                piece = jnp.dot(x_v[:, k], wide_v[t, k], preferred_element_type=jnp.float32)
                both = piece if part == 0 else both + piece
        if t > 0:
            both = jnp.dot(x_v[...], wide_v[t], preferred_element_type=jnp.float32)
        gate, up = both[:, :cols], both[:, cols:]
        out[:, t * cols : (t + 1) * cols] = (gate / (1.0 + jnp.exp(-gate)) * up).astype(jnp.bfloat16)


def down_kernel(cols, hidden, down_m, *refs):
    outs, (down_v, down_sem) = refs[:4], refs[4:]
    width = down_m.shape[1]
    tiles, slots = width // cols, down_v.shape[0]

    def down_copy(t, slot):
        return pltpu.make_async_copy(down_m.at[:, pl.ds(t * cols, cols)], down_v.at[slot], down_sem.at[slot])

    for t in range(slots):
        down_copy(t, t).start()
    for t in range(tiles):
        slot = t % slots
        down_copy(t, slot).wait()
        total = jnp.dot(hidden[...], down_v[slot], preferred_element_type=jnp.float32).astype(jnp.bfloat16)
        first = 0
        for out in outs:
            out[:, t * cols : (t + 1) * cols] = total[first : first + out.shape[0]]
            first += out.shape[0]
        if t + slots < tiles:
            down_copy(t + slots, slot).start()


def in_hbm(matrix):
    return pltpu.with_memory_space_constraint(matrix, pltpu.HBM)


def expert_hidden(blocks, gate_m, up_m):
    rows, width = blocks[0].shape
    hidden = gate_m.shape[1]
    cols, parts = 256, 1
    vmem, stays = pl.BlockSpec(memory_space=pltpu.VMEM), pl.BlockSpec(memory_space=pltpu.HBM)
    return pl.pallas_call(
        functools.partial(hidden_kernel, cols, parts),
        out_shape=jax.ShapeDtypeStruct((8 * rows, hidden), jnp.bfloat16),
        in_specs=[vmem] * 8 + [stays] * 2,
        out_specs=vmem,
        scratch_shapes=[
            pltpu.VMEM((8 * rows, width), jnp.bfloat16),
            pltpu.VMEM((hidden // cols, width, 2 * cols), jnp.bfloat16),
            pltpu.SemaphoreType.DMA((hidden // cols, parts, 2)),
        ],
        compiler_params=pltpu.CompilerParams(vmem_limit_bytes=VMEM_HIDDEN * MIB),
        cost_estimate=pl.CostEstimate(
            flops=32 * rows * width * hidden,
            bytes_accessed=4 * width * hidden + 16 * rows * width,
            transcendentals=8 * rows * hidden,
        ),
        name="expert_hidden",
    )(*blocks, in_hbm(gate_m), in_hbm(up_m))


def expert_down(hidden, down_m):
    rows, width = hidden.shape[0] // 8, down_m.shape[1]
    cols = 1024
    vmem, stays = pl.BlockSpec(memory_space=pltpu.VMEM), pl.BlockSpec(memory_space=pltpu.HBM)
    first, rest = [jax.ShapeDtypeStruct((count * rows, width), jnp.bfloat16) for count in (1, 3)]
    return pl.pallas_call(
        functools.partial(down_kernel, cols),
        out_shape=[first, rest, first, rest],
        in_specs=[vmem, stays],
        out_specs=[vmem] * 4,
        scratch_shapes=[
            pltpu.VMEM((width // cols, down_m.shape[0], cols), jnp.bfloat16),
            pltpu.SemaphoreType.DMA((width // cols,)),
        ],
        compiler_params=pltpu.CompilerParams(vmem_limit_bytes=VMEM_DOWN * MIB),
        cost_estimate=pl.CostEstimate(
            flops=16 * rows * width * down_m.shape[0],
            bytes_accessed=2 * width * down_m.shape[0] + 32 * rows * width,
            transcendentals=0,
        ),
        name="expert_down",
    )(hidden, in_hbm(down_m))


def add(*terms):
    total = terms[0].astype(jnp.float32)
    for term in terms[1:]:
        total += term.astype(jnp.float32)
    return total.astype(jnp.bfloat16)


def after(block, *earlier):
    return lax.optimization_barrier((block, *earlier))[0]


def route(block, target, cores=(0, 1)):
    sections, chips = lax.axis_size("pipe"), lax.axis_size("dp")
    index = lambda section, core, chip: ((section % sections) * 2 + core) * chips + chip
    pairs = [
        (index(section, core, chip), index(*target(section, core, chip)))
        for section in range(sections)
        for core in cores
        for chip in range(chips)
    ]
    return lax.ppermute(block, ("pipe", "expert", "dp"), pairs)


def chip(mask):
    return lambda s, c, z: (s, c, z ^ mask)


def next_chip(mask):
    return lambda s, c, z: (s + 1, c, z ^ mask)


def per_device(hidden_in, norm_gain, w_gate, w_up, w_down, expert_ids, gate_weights):
    rows = hidden_in.shape[0]
    size = rows // 4
    meta, *packed = pack(hidden_in, norm_gain, expert_ids.T, gate_weights.T, [size, size // 2, size // 2])
    meta_before = next_section(meta)
    halves = [packed[0], jnp.concatenate(packed[1:], axis=0)]
    swapped = other_core(packed[0])
    early = after(hidden_in, swapped)

    def hand_on(block, p):
        first = rows * sum(PIECES[:p]) // PIECES_OF
        return next_section(block[first : first + rows * PIECES[p] // PIECES_OF])

    inputs = [hand_on(early, p) for p in range(len(PIECES))]

    def expert_hidden_of(blocks, theirs):
        return expert_hidden(blocks + theirs, w_gate[0], w_up[0])

    def scatter(terms, wait_for_own):
        keep_first, keep_rest, send_first, send_rest = terms
        partner = route(add(keep_first, other_core(send_first)), chip(1))
        rest = add(keep_rest, other_core(send_rest))
        stays = route(rest[2 * size :], next_chip(0))
        across = route(rest[size : 2 * size], next_chip(1))
        if wait_for_own:
            partner = after(partner, stays)
        return [stays, across, route(add(rest[:size], partner), next_chip(3))]

    cross, near = route(packed[0], chip(3)), route(after(packed[0], swapped), chip(1))
    far = route(after(cross, *inputs[:2]), chip(1))
    cross_swapped = other_core(cross)
    cross_next = [route(after(block, cross_swapped), chip(3)) for block in packed[1:]]
    near_next = route(after(halves[1], cross_swapped, cross_next[0]), chip(1))
    mine = [far, cross, near, after(packed[0], inputs[2], cross_next[0], meta_before)]
    hidden = expert_hidden_of(mine, [other_core(far), cross_swapped, other_core(near), swapped])
    cross_next = jnp.concatenate([after(block, hidden) for block in cross_next], axis=0)
    far_next = route(after(cross_next, hidden), chip(1))
    keep_first, keep_rest, send_first, send_rest = expert_down(after(hidden, near_next, inputs[3]), w_down[0])
    send_first, send_rest = after(send_first, far_next), after(send_rest, far_next)
    arrived = scatter([keep_first, keep_rest, send_first, send_rest], True)

    mine = [far_next, cross_next, near_next, halves[1]]
    hidden = expert_hidden_of(mine, [other_core(block) for block in mine])
    keep_first, keep_rest, send_first, send_rest = expert_down(hidden, w_down[0])
    send_first, send_rest = after(send_first, *arrived), after(send_rest, *arrived)
    arrived += scatter([keep_first, keep_rest, send_first, send_rest], False)
    return combine(inputs, meta_before, arrived)


def rms_scale(values_in, gain):
    values = values_in.astype(jnp.float32)
    mean_sq = jnp.mean(values * values, axis=-1, keepdims=True)
    return (values * lax.rsqrt(mean_sq + 1e-05) * gain).astype(jnp.bfloat16)


def expert_rows(normed, gate_matrix, up_matrix, down_matrix):
    gate = jnp.dot(normed, gate_matrix, preferred_element_type=jnp.float32)
    up_values = jnp.dot(normed, up_matrix, preferred_element_type=jnp.float32)
    hidden = (jax.nn.silu(gate) * up_values).astype(jnp.bfloat16)
    return jnp.dot(hidden, down_matrix, preferred_element_type=jnp.float32)


def per_device_any(hidden_in, norm_gain, w_gate, w_up, w_down, expert_ids, gate_weights):
    row_count = hidden_in.shape[0]
    capacity = row_count // 2
    normed = rms_scale(hidden_in, norm_gain[0])
    chosen = expert_ids == 0
    routed = jnp.any(chosen, axis=1)
    own_weight = jnp.sum(jnp.where(chosen, gate_weights, 0.0), axis=1)
    position = jnp.cumsum(routed.astype(jnp.int32)) - 1
    slot_grid = lax.broadcasted_iota(jnp.int32, (capacity, row_count), 0)
    token_grid = lax.broadcasted_iota(jnp.int32, (capacity, row_count), 1)
    picked = (position[None, :] == slot_grid) & routed[None, :]
    source = jnp.sum(jnp.where(picked, token_grid, 0), axis=1)
    filled = jnp.any(picked, axis=1)
    packed = jnp.where(
        filled[:, None], jnp.take(normed, source, axis=0), jnp.zeros_like(normed[:1])
    )
    gate_matrix = w_gate[0]
    up_matrix = w_up[0]
    down_matrix = w_down[0]
    terms = expert_rows(
        lax.all_gather(packed, ("expert", "dp"), axis=0, tiled=True),
        gate_matrix,
        up_matrix,
        down_matrix,
    )
    own_rows = lax.psum_scatter(
        terms.astype(jnp.bfloat16), ("expert", "dp"), scatter_dimension=0, tiled=True
    ).astype(jnp.float32)
    back = jnp.take(own_rows, jnp.clip(position, 0, capacity - 1), axis=0)
    branch = jnp.where(routed[:, None], back, 0.0)
    combined = (hidden_in.astype(jnp.float32) + own_weight[:, None] * branch).astype(jnp.bfloat16)
    return next_section(combined)


def solution(mesh):
    paired = mesh.shape["dp"] == 4 and mesh.shape["expert"] == 2
    return jax.shard_map(
        per_device if paired else per_device_any,
        mesh=mesh,
        in_specs=(
            P(("pipe", "expert", "dp"), None),
            P("pipe", None),
            P("pipe", None, ("expert", "dp")),
            P("pipe", None, ("expert", "dp")),
            P("pipe", ("expert", "dp"), None),
            P(("pipe", "expert", "dp"), None),
            P(("pipe", "expert", "dp"), None),
        ),
        out_specs=P(("pipe", "expert", "dp"), None),
        check_vma=False,
    )
```
